32 devices in a mesh: groups: 2 (over y), rows: 4 (over z), tiles: 2 (over x), sub: 2 (over core).
Axes of the slice: x: 2, y: 2, z: 4, core: 2. Of those that a mesh axis runs over, the one named last changes fastest.
Arguments:
- points: float32 [20480, 64], P(('groups', 'rows')), parts along dimension 0, may hold values from -6 to 6
- targets: float32 [20480, 128], P(('groups', 'rows', 'tiles', 'sub')), parts along dimension 0, may hold values from -6 to 6
- pair_list: int32 [32, 2, 25], P(('groups', 'rows', 'tiles', 'sub')), parts along dimension 0, may hold values from -1 to 19, as said below
Outputs:
- solution: float32 [20480, 128], P(('groups', 'rows', 'tiles', 'sub')), parts along dimension 0
- residual: float32 [20480, 128], P(('groups', 'rows', 'tiles', 'sub')), parts along dimension 0
The draws below stay inside these ranges and needn't reach their ends.
There are 2 independent parts, one for each index of `groups`. The reference program is written for one: setup_inputs(seed, part) draws one part's arguments, and reference() takes and returns one part's arrays. A program takes and returns all parts, laid end to end along the dimension named above; each array names one. Nothing has to cross between parts.
Inputs may be any that keep to these rules, and one draw needn't show every extreme that they name: Holder h lies in row group h // 4. Slot k of holder h is the pair i = pair_list[h, 0, k], j = pair_list[h, 1, k] with i in that row group and i <= j <= i + 4, j < 20. A holder's live pairs come first and the remaining slots hold -1 in both rows. Every pair appears at most once over all holders, and every diagonal pair (i, i) appears.
All inputs are finite; a program needn't handle non-finite values.
Results may differ from the reference program's by a relative error of at most 0.0024.
Values may be sent and summed in bfloat16 or wider, within the bound.
A program may use at most 64 MiB of HBM per device.

```python
import math
import jax
import jax.numpy as jnp
from jax import lax

F = 64
COLS = 128
BLOCK_POINTS = 512
BPR = 5
REACH = 4
ITERS = 2
NB = 20
NPTS = 10240
HOLDERS = 16
CAP = 25
N_ROWS = 4
N_TILES = 2
N_SUB = 2


def block_coord(key):
    gap_key = jax.random.fold_in(key, 3)
    gaps = 1 + (jax.random.randint(gap_key, (NB,), 0, 4) == 3).astype(jnp.int32)
    return jnp.cumsum(gaps) - gaps[0]


def draw_points(key, part):
    coord = block_coord(key).astype(jnp.float32)
    key = jax.random.fold_in(key, 5)
    keys = jax.random.split(key, 6)
    feature_scale = jnp.exp(jax.random.uniform(keys[0], (1, F), jnp.float32, math.log(0.01), 0.0))
    freq = jnp.exp(jax.random.uniform(keys[1], (1, F), jnp.float32, math.log(0.06), math.log(0.22)))
    phase = jax.random.uniform(keys[2], (1, F), jnp.float32, -math.pi, math.pi)
    jitter = jax.random.uniform(keys[3], (NPTS, 1), jnp.float32, 0.0, 1.0)
    spread = jnp.exp(jax.random.uniform(keys[4], (NPTS, 1), jnp.float32, math.log(0.3), math.log(2.5)))
    index = jnp.arange(NPTS, dtype=jnp.int32)
    place = coord[index // BLOCK_POINTS][:, None] + jitter
    curve = 4.5 * jnp.cos(freq * place + phase)
    noise = jnp.clip(jax.random.normal(keys[5], (NPTS, F), jnp.float32), -4.0, 4.0)
    return jnp.clip(feature_scale * (curve + spread * noise), -6.0, 6.0)


def draw_targets(key, part):
    coord = block_coord(key).astype(jnp.float32)
    key = jax.random.fold_in(key, 7)
    keys = jax.random.split(key, 5)
    index = jnp.arange(NPTS, dtype=jnp.int32)
    place = coord[index // BLOCK_POINTS] + (index % BLOCK_POINTS).astype(jnp.float32) / BLOCK_POINTS
    ramp = (index.astype(jnp.float32) / NPTS)[:, None]
    amp = jnp.exp(jax.random.uniform(keys[0], (1, COLS), jnp.float32, math.log(0.1), 0.0))
    freq = jnp.exp(jax.random.uniform(keys[1], (1, COLS), jnp.float32, math.log(0.05), math.log(0.5)))
    phase = jax.random.uniform(keys[2], (1, COLS), jnp.float32, -math.pi, math.pi)
    smooth = amp * jnp.sin(freq * place[:, None] + phase)
    rough = jnp.clip(jax.random.normal(keys[4], (NPTS, COLS), jnp.float32), -4.0, 4.0) * (1.0 + 0.75 * ramp)
    return jnp.clip(smooth + rough, -6.0, 6.0)


def draw_pair_list(key, part):
    coord = block_coord(key)
    key = jax.random.fold_in(key, 11)
    favor_key, coin_key, other_key = jax.random.split(key, 3)
    group_holders = N_TILES * N_SUB
    first = jnp.broadcast_to(jnp.arange(NB, dtype=jnp.int32)[:, None], (NB, REACH + 1))
    second = first + jnp.arange(REACH + 1, dtype=jnp.int32)[None, :]
    inside = second < NB
    second_coord = coord[jnp.minimum(second, NB - 1)]
    valid = inside & (second_coord - coord[:, None] <= REACH)
    favored = jax.random.randint(favor_key, (N_ROWS,), 0, group_holders)
    coin = jax.random.randint(coin_key, (NB, REACH + 1), 0, 8)
    other = jax.random.randint(other_key, (NB, REACH + 1), 0, group_holders)
    owner = jnp.where(coin < 3, favored[first // BPR], other)
    first_g = first.reshape(N_ROWS, 1, CAP)
    second_g = second.reshape(N_ROWS, 1, CAP)
    match = valid.reshape(N_ROWS, 1, CAP) & (owner.reshape(N_ROWS, 1, CAP) == jnp.arange(group_holders, dtype=jnp.int32)[None, :, None])
    position = jnp.arange(CAP, dtype=jnp.int32)[None, None, :]
    order = jnp.argsort(jnp.where(match, position, position + CAP), axis=-1)
    count = jnp.sum(match.astype(jnp.int32), axis=-1)
    live = position < count[:, :, None]
    left = jnp.take_along_axis(jnp.broadcast_to(first_g, match.shape), order, axis=-1)
    right = jnp.take_along_axis(jnp.broadcast_to(second_g, match.shape), order, axis=-1)
    left = jnp.where(live, left, -1)
    right = jnp.where(live, right, -1)
    return jnp.stack([left, right], axis=2).reshape(HOLDERS, 2, CAP).astype(jnp.int32)


def setup_inputs(seed: int = 0, part: int = 0) -> dict:
    key_of = jax.random.split(jax.random.key(seed), 4)
    own_keys = jax.random.split(jax.random.fold_in(key_of[3], part), 4)
    points = draw_points(jax.random.fold_in(jax.random.fold_in(key_of[3], part), 71), part)
    targets = draw_targets(jax.random.fold_in(jax.random.fold_in(key_of[3], part), 71), part)
    pair_list = draw_pair_list(jax.random.fold_in(jax.random.fold_in(key_of[3], part), 71), part)
    return {"points": points, "targets": targets, "pair_list": pair_list}


support_radius = 12.0
noise_variance = 0.25
highest = lax.Precision.HIGHEST

def kernel_tile(left_pts, right_pts, left_sq, right_sq):
    inner = lax.dot_general(left_pts, right_pts, (((1,), (1,)), ((), ())), precision=highest, preferred_element_type=jnp.float32)
    dist_sq = left_sq[:, None] + right_sq[None, :] - 2.0 * inner
    radius = jnp.sqrt(jnp.maximum(dist_sq, 0.0)) / support_radius
    base = jnp.maximum(1.0 - radius, 0.0)
    base_sq = base * base
    return (base_sq * base_sq * (4.0 * radius + 1.0)).astype(jnp.bfloat16)

def reference(points, targets, pair_list):
    left_all = pair_list[:, 0, :].reshape(-1)
    right_all = pair_list[:, 1, :].reshape(-1)
    total = left_all.shape[0]
    slot = jnp.arange(total, dtype=jnp.int32)
    order = jnp.argsort(jnp.where(left_all >= 0, slot, slot + total))
    left_all = left_all[order].astype(jnp.int32)
    right_all = right_all[order].astype(jnp.int32)
    count = jnp.sum((left_all >= 0).astype(jnp.int32))
    point_sq = lax.optimization_barrier(jnp.sum(points * points, axis=1))
    kernel_amplitude = 1.0 / BLOCK_POINTS

    def apply_matrix(search_direction):
        dir16 = search_direction.astype(jnp.bfloat16)

        def one_tile(k, running_total):
            left = left_all[k]
            right = right_all[k]
            left_start = (left * BLOCK_POINTS).astype(jnp.int32)
            right_start = (right * BLOCK_POINTS).astype(jnp.int32)
            tile = kernel_tile(lax.dynamic_slice_in_dim(points, left_start, BLOCK_POINTS, 0), lax.dynamic_slice_in_dim(points, right_start, BLOCK_POINTS, 0), lax.dynamic_slice_in_dim(point_sq, left_start, BLOCK_POINTS, 0), lax.dynamic_slice_in_dim(point_sq, right_start, BLOCK_POINTS, 0)).astype(jnp.float32)
            left_dir = lax.dynamic_slice_in_dim(dir16, left_start, BLOCK_POINTS, 0).astype(jnp.float32)
            right_dir = lax.dynamic_slice_in_dim(dir16, right_start, BLOCK_POINTS, 0).astype(jnp.float32)
            to_left = jnp.dot(tile, right_dir, precision=highest)
            to_right = lax.dot_general(tile, left_dir, (((0,), (0,)), ((), ())), precision=highest)
            off_diag = (left != right).astype(jnp.float32)
            running_total = lax.dynamic_update_slice_in_dim(running_total, lax.dynamic_slice_in_dim(running_total, left_start, BLOCK_POINTS, 0) + to_left, left_start, 0)
            running_total = lax.dynamic_update_slice_in_dim(running_total, lax.dynamic_slice_in_dim(running_total, right_start, BLOCK_POINTS, 0) + off_diag * to_right, right_start, 0)
            return running_total
        running_total = lax.fori_loop(0, count, one_tile, jnp.zeros(search_direction.shape, jnp.float32))
        return noise_variance * search_direction + running_total * kernel_amplitude
    solution = jnp.zeros(targets.shape, jnp.float32)
    residual = targets
    search_direction = targets
    norm_now = lax.optimization_barrier(jnp.sum(residual * residual, axis=0))
    for step in range(ITERS):
        kernel_times_direction = apply_matrix(search_direction)
        alpha = norm_now / lax.optimization_barrier(jnp.sum(search_direction * kernel_times_direction, axis=0))
        solution = solution + alpha * search_direction
        residual = residual - alpha * kernel_times_direction
        if step + 1 < ITERS:
            norm_next = lax.optimization_barrier(jnp.sum(residual * residual, axis=0))
            search_direction = residual + norm_next / norm_now * search_direction
            norm_now = norm_next
    return (solution, residual)
```

```python
import functools

import jax
import jax.numpy as jnp
from jax import lax
from jax.experimental import pallas as pl
from jax.experimental.pallas import tpu as pltpu
from jax.sharding import PartitionSpec as P

BLOCK = 512
HALF = 256
HROWS = 272
REACH = 4
SLOTS = 13
f32 = jnp.float32
bf16 = jnp.bfloat16


def split(v):
    hi = lax.reduce_precision(v, 8, 7)
    return hi, v - hi


def pack_points(points):
    hi, rest = split(points)
    lo = lax.reduce_precision(rest, 8, 7)
    both = hi + lo
    sq = jnp.sum(both * both, axis=1)
    n1, rest = split(sq)
    n2, n3 = split(rest)
    blocks = points.shape[0] // BLOCK
    feats = jnp.concatenate([hi, lo], axis=1).astype(bf16).reshape(blocks, 2, HALF, 128)
    pieces = jnp.stack([n1, n2, n3], axis=0).reshape(3, blocks, 2, 2, 128)
    pieces = pieces.transpose(1, 2, 3, 0, 4).reshape(blocks, 2, 6, 128)
    pieces = jnp.pad(pieces, ((0, 0), (0, 0), (0, 10), (0, 0))).astype(bf16)
    return jnp.concatenate([feats, pieces], axis=2)


def kernel(nz, nx, cap, tgt, pts, pairs, sol, res, pbuf, d0, d1, kbuf, abuf, na, acc, r1, dir2,
           pres, prevp, red1, red2, loc, gs, gr, gf, pzs, pzr, pfs, pfr, dzs, dzr, dfs, dfr,
           prs, prr, qs, qr, r1s, r1r, r2s, r2r):
    T = nx * 2
    R = tgt.shape[0]
    U = BLOCK // T
    UPH = T // 2
    x = lax.axis_index("tiles")
    c = lax.axis_index("sub")
    z = lax.axis_index("rows")
    t = x * 2 + c
    b0 = (5 * t) // T
    b1 = (5 * t + 4) // T
    b0c = (10 * x) // T
    b1c = (10 * x + 9) // T
    has_prev = z > 0
    has_next = z < nz - 1

    def partner():
        return {"sub": 1 - c}

    def have(e):
        if e < 4:
            return jnp.logical_and(has_prev, e + 1 >= b0c + 1)
        return jnp.logical_and(has_next, e - 9 <= b1c - 1)

    def rcopy(src, dst, s, r, dev):
        return pltpu.make_async_remote_copy(
            src_ref=src, dst_ref=dst, send_sem=s, recv_sem=r, device_id=dev,
            device_id_type=pl.DeviceIdType.MESH)

    EXT = (3, 9, 2, 10, 1, 11, 0, 12)

    own_rows = pl.ds(pl.multiple_of(REACH * BLOCK + t * R, 64), R)
    lc = pltpu.make_async_copy(pts, pbuf.at[pl.ds(4, 5)], loc)
    lc.start()
    d0[own_rows, :] = tgt[...].astype(bf16)
    lane = lax.broadcasted_iota(jnp.int32, (1, 128), 1)
    mine = jnp.zeros((1, 128), f32)
    for k in range(cap):
        left = pairs[0, 0, k]
        right = pairs[0, 1, k]
        code = jnp.where(left >= 0, (left - z * 5) * 5 + right - left, -100)
        hit = jnp.logical_or(lane == code, lane == code + 25)
        mine = jnp.where(hit, 1.0, mine)
    pres[t] = jnp.broadcast_to(mine, (8, 128))

    bar = pltpu.get_barrier_semaphore()

    def mates():
        for o in range(1, T):
            ot = lax.rem(t + o, T)
            yield o, ot, {"tiles": ot // 2, "sub": lax.rem(ot, 2)}

    def ranks():
        for o in range(1, nz):
            oz = lax.rem(z + o, nz)
            yield o, oz, {"rows": oz}

    for _, _, dev in mates():
        pl.semaphore_signal(bar, inc=1, device_id=dev, device_id_type=pl.DeviceIdType.MESH)
    for _, _, dev in ranks():
        pl.semaphore_signal(bar, inc=1, device_id=dev, device_id_type=pl.DeviceIdType.MESH)
    pl.semaphore_wait(bar, T - 1 + nz - 1)

    def gather_copies(it, d):
        view = d.at[own_rows]
        out = [rcopy(view, view, gs.at[it, 0], gr.at[it, t], partner())]
        for o in range(1, nx):
            out.append(rcopy(view, view, gs.at[it, o], gr.at[it, t], {"tiles": lax.rem(x + o, nx)}))
        return out

    def gather_from(it, d, o):
        src_t = lax.rem(x + nx - o, nx) * 2 + c
        rows = pl.ds(pl.multiple_of(REACH * BLOCK + src_t * R, 64), R)
        return (rcopy(d.at[rows], d.at[rows], gs.at[it, o], gr.at[it, src_t], partner()),
                rcopy(d.at[rows], d.at[rows], gf.at[it, o], gr.at[it, src_t], partner()))

    def gather_forward(it, d):
        for o in range(1, nx):
            inn, fwd = gather_from(it, d, o)
            inn.wait_recv()
            fwd.start()

    def gather_wait(it, d):
        for xx in range(nx):
            src_t = xx * 2 + (1 - c)
            rows = pl.ds(pl.multiple_of(REACH * BLOCK + src_t * R, 64), R)
            rcopy(d.at[rows], d.at[rows], gs.at[it, 0], gr.at[it, src_t], partner()).wait_recv()

    def p_send(e):
        if e < 4:
            return rcopy(pts.at[e + 1, c], pbuf.at[e, c], pzs.at[e], pzr.at[e], {"rows": z + 1})
        return rcopy(pts.at[e - 9, c], pbuf.at[e, c], pzs.at[e], pzr.at[e], {"rows": z - 1})

    def can_send(e):
        if e < 4:
            return jnp.logical_and(has_next, e + 1 >= b0c + 1)
        return jnp.logical_and(has_prev, e - 9 <= b1c - 1)

    def p_fwd(e):
        return rcopy(pbuf.at[e, c], pbuf.at[e, c], pfs.at[e], pfr.at[e], partner())

    def half_rows(e, h):
        return pl.ds(pl.multiple_of(e * BLOCK + h * HALF, HALF), HALF)

    def d_send(it, d, e):
        s = e + 5 if e < 4 else e - 5
        dev = {"rows": z + 1} if e < 4 else {"rows": z - 1}
        return rcopy(d.at[half_rows(s, c)], d.at[half_rows(e, c)], dzs.at[it, e], dzr.at[it, e], dev)

    def d_fwd(it, d, e):
        v = d.at[half_rows(e, c)]
        return rcopy(v, v, dfs.at[it, e], dfr.at[it, e], partner())

    def d_fwd_in(it, d, e):
        v = d.at[half_rows(e, 1 - c)]
        return rcopy(v, v, dfs.at[it, e], dfr.at[it, e], partner())

    def pfwd_in(e):
        v = pbuf.at[e, 1 - c]
        return rcopy(v, v, pfs.at[e], pfr.at[e], partner())

    def each(cond, fn):
        for e in EXT:
            @pl.when(cond(e))
            def _(e=e):
                fn(e)

    pc = [rcopy(pres.at[t], pres.at[t], prs.at[o], prr.at[t], dev) for o, _, dev in mates()]
    for cp in pc:
        cp.start()
    for cp in gather_copies(0, d0):
        cp.start()
    each(can_send, lambda e: p_send(e).start())
    lc.wait()

    for k in range(5):
        g = 5 * t + k
        hb = g // UPH
        off = pl.multiple_of(lax.rem(g, UPH) * U, U)
        rows = pbuf[4 + hb // 2, lax.rem(hb, 2), pl.ds(off, U), :].astype(f32)
        turned = pltpu.roll(rows, 64, 1)
        abuf[k * U:(k + 1) * U, 0:128] = (-2.0 * rows).astype(bf16)
        abuf[k * U:(k + 1) * U, 128:256] = (-2.0 * turned).astype(bf16)
        na[k * U:(k + 1) * U, :] = jnp.broadcast_to(
            jnp.sum(rows * (rows + turned), axis=1, keepdims=True), (U, 128))

    for o, ot, dev in mates():
        rcopy(pres.at[ot], pres.at[ot], prs.at[o], prr.at[ot], dev).wait_recv()
    own = pres[0]
    for i in range(1, T):
        own = own + pres[i]
    prevp[1] = jnp.where(lane >= 25, own, 0.0)
    prevp[2] = jnp.where(lane < 25, own, 0.0)

    def q_copy():
        return rcopy(prevp.at[2], prevp.at[0], qs, qr, {"rows": z + 1})

    @pl.when(has_next)
    def _():
        q_copy().start()

    @pl.when(jnp.logical_not(has_prev))
    def _():
        prevp[0] = jnp.zeros((8, 128), f32)

    def build(e, listed):
        for h in range(2):
            blk = pbuf[e, h]
            b = blk[:HALF]
            nr = blk[HALF:].astype(f32)
            nc = jnp.concatenate([nr[0:1] + nr[1:2] + nr[2:3], nr[3:4] + nr[4:5] + nr[5:6]], axis=1)
            gram = lax.dot_general(abuf[...], jnp.concatenate([b, b], axis=1),
                                   (((1,), (1,)), ((), ())), preferred_element_type=f32)
            for k in range(5):
                i = (5 * t + k) // T
                j = e - 4
                dist = jnp.abs(i - j)
                code = jnp.where(dist <= REACH, (jnp.minimum(i, j) + 5) * 5 + dist, 127)
                m = jnp.sum(jnp.where(lane == code, listed, 0.0), axis=1, keepdims=True)
                u = slice(k * U, (k + 1) * U)
                s = gram[u] + nc + na[u, 0:1]
                s = jnp.maximum(s, 1e-20)
                r = s * lax.rsqrt(s) * (1.0 / 12.0)
                base = jnp.maximum(m - r, 0.0)
                base2 = base * base
                kt = base2 * base2 * (4.0 * r + 1.0)
                kbuf[e - b0, u, h * HALF:(h + 1) * HALF] = kt.astype(bf16)

    def builds(lo, hi, listed):
        def body(e, carry):
            build(e, listed)
            return carry
        lax.fori_loop(lo, hi, body, 0)

    def mults(d, lo, hi):
        def body(e, carry):
            acc[...] += jnp.dot(kbuf[e - b0], d[pl.ds(pl.multiple_of(e * BLOCK, BLOCK), BLOCK), :],
                                preferred_element_type=f32)
            return carry
        lax.fori_loop(lo, hi, body, 0)

    prev_lo = jnp.where(has_prev, b0, 4)
    next_hi = jnp.where(has_next, b1 + 9, 9)

    own_list = jnp.minimum(prevp[1, 0:1], 1.0)
    acc[...] = jnp.zeros_like(acc)
    builds(4, 6, own_list)
    gather_forward(0, d0)
    builds(6, 7, own_list)
    gather_wait(0, d0)
    each(can_send, lambda e: d_send(0, d0, e).start())
    builds(7, 9, own_list)

    def p_take(e):
        p_send(e).wait_recv()
        p_fwd(e).start()

    each(have, p_take)
    mults(d0, 4, 9)

    @pl.when(has_prev)
    def _():
        q_copy().wait_recv()
    each(have, lambda e: pfwd_in(e).wait_recv())
    whole_list = jnp.minimum(prevp[1, 0:1] + prevp[0, 0:1], 1.0)
    builds(prev_lo, 4, whole_list)
    builds(9, next_hi, whole_list)

    def d_finish(it, d):
        def take(e):
            d_send(it, d, e).wait_recv()
            d_fwd(it, d, e).start()
        each(have, take)
        each(have, lambda e: d_fwd_in(it, d, e).wait_recv())
        mults(d, prev_lo, 4)
        mults(d, 9, next_hi)

    d_finish(0, d0)

    def total(it, sums):
        rows = [*sums] + [jnp.zeros((8 - len(sums), 128), f32)]
        red1[it, t] = jnp.concatenate(rows, axis=0)
        v = red1.at[it, t]
        for o, ot, dev in mates():
            rcopy(v, v, r1s.at[it, o], r1r.at[it, t], dev).start()
        for o, ot, dev in mates():
            w = red1.at[it, ot]
            rcopy(w, w, r1s.at[it, o], r1r.at[it, ot], dev).wait_recv()
        a = red1[it, 0]
        for i in range(1, T):
            a = a + red1[it, i]
        red2[it, z] = a
        v = red2.at[it, z]
        for o, oz, dev in ranks():
            rcopy(v, v, r2s.at[it, o], r2r.at[it, z], dev).start()
        for o, oz, dev in ranks():
            w = red2.at[it, oz]
            rcopy(w, w, r2s.at[it, o], r2r.at[it, oz], dev).wait_recv()
        a = red2[it, 0]
        for i in range(1, nz):
            a = a + red2[it, i]
        return a

    def colsum(v):
        return jnp.sum(v, axis=0, keepdims=True)

    tv = tgt[...]
    q = 0.25 * tv + acc[...] * (1.0 / BLOCK)
    sums = total(0, (colsum(tv * tv), colsum(tv * q), colsum(q * q)))
    rr, tq, qq = sums[0:1], sums[1:2], sums[2:3]
    alpha = rr / tq
    beta = (alpha * alpha * qq - rr) / rr
    q = 0.25 * tgt[...] + acc[...] * (1.0 / BLOCK)
    first = tgt[...] - alpha * q
    r1[...] = first
    second = first + beta * tgt[...]
    dir2[...] = second
    d1[own_rows, :] = second.astype(bf16)
    for cp in gather_copies(1, d1):
        cp.start()
    acc[...] = jnp.zeros_like(acc)
    gather_forward(1, d1)
    gather_wait(1, d1)
    each(can_send, lambda e: d_send(1, d1, e).start())
    mults(d1, 4, 9)
    d_finish(1, d1)
    q = 0.25 * dir2[...] + acc[...] * (1.0 / BLOCK)
    sums = total(1, (colsum(r1[...] * r1[...]), colsum(dir2[...] * q)))
    alpha2 = sums[0:1] / sums[1:2]
    q = 0.25 * dir2[...] + acc[...] * (1.0 / BLOCK)
    sol[...] = alpha * tgt[...] + alpha2 * dir2[...]
    res[...] = r1[...] - alpha2 * q

    for cp in pc:
        cp.wait_send()

    @pl.when(has_next)
    def _():
        q_copy().wait_send()
    each(can_send, lambda e: p_send(e).wait_send())
    each(have, lambda e: p_fwd(e).wait_send())
    for it, d in enumerate((d0, d1)):
        for cp in gather_copies(it, d):
            cp.wait_send()
        for o in range(1, nx):
            gather_from(it, d, o)[1].wait_send()
        each(can_send, lambda e: d_send(it, d, e).wait_send())
        each(have, lambda e: d_fwd(it, d, e).wait_send())
        for o, ot, dev in mates():
            rcopy(red1.at[it, t], red1.at[it, t], r1s.at[it, o], r1r.at[it, t], dev).wait_send()
        for o, oz, dev in ranks():
            rcopy(red2.at[it, z], red2.at[it, z], r2s.at[it, o], r2r.at[it, z], dev).wait_send()


def local(nz, nx, points, targets, pair_list):
    T = nx * 2
    R = targets.shape[0]
    pts = pack_points(points)
    dma = pltpu.SemaphoreType.DMA
    vmem = pl.BlockSpec(memory_space=pltpu.VMEM)
    shape = jax.ShapeDtypeStruct(targets.shape, f32)
    return pl.pallas_call(
        functools.partial(kernel, nz, nx, pair_list.shape[2]),
        out_shape=(shape, shape),
        in_specs=[vmem, pl.BlockSpec(memory_space=pl.ANY), pl.BlockSpec(memory_space=pltpu.SMEM)],
        out_specs=(vmem, vmem),
        scratch_shapes=[
            pltpu.VMEM((SLOTS, 2, HROWS, 128), bf16),
            pltpu.VMEM((SLOTS * BLOCK, 128), bf16),
            pltpu.VMEM((SLOTS * BLOCK, 128), bf16),
            pltpu.VMEM((10, R, BLOCK), bf16),
            pltpu.VMEM((R, 256), bf16),
            pltpu.VMEM((R, 128), f32),
            pltpu.VMEM((R, 128), f32),
            pltpu.VMEM((R, 128), f32),
            pltpu.VMEM((R, 128), f32),
            pltpu.VMEM((T, 8, 128), f32),
            pltpu.VMEM((3, 8, 128), f32),
            pltpu.VMEM((2, T, 8, 128), f32),
            pltpu.VMEM((2, nz, 8, 128), f32),
            dma,
            dma((2, nx)), dma((2, T)), dma((2, nx)),
            dma((SLOTS,)), dma((SLOTS,)), dma((SLOTS,)), dma((SLOTS,)),
            dma((2, SLOTS)), dma((2, SLOTS)), dma((2, SLOTS)), dma((2, SLOTS)),
            dma((T,)), dma((T,)), dma, dma,
            dma((2, T)), dma((2, T)), dma((2, nz)), dma((2, nz)),
        ],
        compiler_params=pltpu.CompilerParams(
            collective_id=0, has_side_effects=True, vmem_limit_bytes=48 * 1024 * 1024),
        cost_estimate=pl.CostEstimate(flops=5 * 10**9, bytes_accessed=2 * 10**6, transcendentals=3 * 10**6),
    )(targets, pts, pair_list)


def solution(mesh):
    nz, nx = mesh.shape["rows"], mesh.shape["tiles"]
    in_specs = (
        P(("groups", "rows"), None),
        P(("groups", "rows", "tiles", "sub"), None),
        P(("groups", "rows", "tiles", "sub"), None, None),
    )
    out_specs = (
        P(("groups", "rows", "tiles", "sub"), None),
        P(("groups", "rows", "tiles", "sub"), None),
    )
    return jax.shard_map(functools.partial(local, nz, nx), mesh=mesh, in_specs=in_specs,
                         out_specs=out_specs, check_vma=False)
```

```python
import functools

import jax
import jax.numpy as jnp
from jax import lax
from jax.experimental import pallas as pl
from jax.experimental.pallas import tpu as pltpu
from jax.sharding import PartitionSpec as P

BLOCK = 512
HALF = 256
HROWS = 272
REACH = 4
SLOTS = 13
f32 = jnp.float32
bf16 = jnp.bfloat16


def split(v):
    hi = lax.reduce_precision(v, 8, 7)
    return hi, v - hi


def pack_points(points):
    hi, rest = split(points)
    lo = lax.reduce_precision(rest, 8, 7)
    both = hi + lo
    sq = jnp.sum(both * both, axis=1)
    n1, rest = split(sq)
    n2, n3 = split(rest)
    blocks = points.shape[0] // BLOCK
    feats = jnp.concatenate([hi, lo], axis=1).astype(bf16).reshape(blocks, 2, HALF, 128)
    pieces = jnp.stack([n1, n2, n3], axis=0).reshape(3, blocks, 2, 2, 128)
    pieces = pieces.transpose(1, 2, 3, 0, 4).reshape(blocks, 2, 6, 128)
    pieces = jnp.pad(pieces, ((0, 0), (0, 0), (0, 10), (0, 0))).astype(bf16)
    return jnp.concatenate([feats, pieces], axis=2)


def kernel(nz, nx, cap, tgt, pts, pairs, sol, res, pbuf, d0, d1, kbuf, abuf, na, acc, r1, dir2,
           pres, prevp, red1, red2, loc, gs, gr, gf, pzs, pzr, pfs, pfr, dzs, dzr, dfs, dfr,
           prs, prr, qs, qr, r1s, r1r, r2s, r2r):
    T = nx * 2
    R = tgt.shape[0]
    U = BLOCK // T
    UPH = T // 2
    x = lax.axis_index("tiles")
    c = lax.axis_index("sub")
    z = lax.axis_index("rows")
    t = x * 2 + c
    b0 = (5 * t) // T
    b1 = (5 * t + 4) // T
    b0c = (10 * x) // T
    b1c = (10 * x + 9) // T
    has_prev = z > 0
    has_next = z < nz - 1

    def partner():
        return {"sub": 1 - c}

    def have(e):
        if e < 4:
            return jnp.logical_and(has_prev, e + 1 >= b0c + 1)
        return jnp.logical_and(has_next, e - 9 <= b1c - 1)

    def rcopy(src, dst, s, r, dev):
        return pltpu.make_async_remote_copy(
            src_ref=src, dst_ref=dst, send_sem=s, recv_sem=r, device_id=dev,
            device_id_type=pl.DeviceIdType.MESH)

    EXT = (3, 9, 2, 10, 1, 11, 0, 12)

    own_rows = pl.ds(pl.multiple_of(REACH * BLOCK + t * R, 64), R)
    lc = pltpu.make_async_copy(pts, pbuf.at[pl.ds(4, 5)], loc)
    lc.start()
    d0[own_rows, :] = tgt[...].astype(bf16)
    lane = lax.broadcasted_iota(jnp.int32, (1, 128), 1)
    mine = jnp.zeros((1, 128), f32)
    for k in range(cap):
        left = pairs[0, 0, k]
        right = pairs[0, 1, k]
        code = jnp.where(left >= 0, (left - z * 5) * 5 + right - left, -100)
        hit = jnp.logical_or(lane == code, lane == code + 25)
        mine = jnp.where(hit, 1.0, mine)
    pres[t] = jnp.broadcast_to(mine, (8, 128))

    bar = pltpu.get_barrier_semaphore()

    def mates():
        for o in range(1, T):
            ot = lax.rem(t + o, T)
            yield o, ot, {"tiles": ot // 2, "sub": lax.rem(ot, 2)}

    def ranks():
        for o in range(1, nz):
            oz = lax.rem(z + o, nz)
            yield o, oz, {"rows": oz}

    flat = T * nz <= 16
    me = z * T + t

    def others():
        for o in range(1, T * nz):
            m = lax.rem(me + o, T * nz)
            yield o, m, {"rows": m // T, "tiles": lax.rem(m, T) // 2, "sub": lax.rem(m, 2)}

    greeted = list(others()) if flat else [*mates(), *ranks()]
    for _, _, dev in greeted:
        pl.semaphore_signal(bar, inc=1, device_id=dev, device_id_type=pl.DeviceIdType.MESH)
    pl.semaphore_wait(bar, len(greeted))

    def gather_copies(it, d):
        view = d.at[own_rows]
        out = [rcopy(view, view, gs.at[it, 0], gr.at[it, t], partner())]
        for o in range(1, nx):
            out.append(rcopy(view, view, gs.at[it, o], gr.at[it, t], {"tiles": lax.rem(x + o, nx)}))
        return out

    def gather_from(it, d, o):
        src_t = lax.rem(x + nx - o, nx) * 2 + c
        rows = pl.ds(pl.multiple_of(REACH * BLOCK + src_t * R, 64), R)
        return (rcopy(d.at[rows], d.at[rows], gs.at[it, o], gr.at[it, src_t], partner()),
                rcopy(d.at[rows], d.at[rows], gf.at[it, o], gr.at[it, src_t], partner()))

    def gather_forward(it, d):
        for o in range(1, nx):
            inn, fwd = gather_from(it, d, o)
            inn.wait_recv()
            fwd.start()
            d_start(it, d, o)

    def gather_wait(it, d):
        for xx in range(nx):
            src_t = xx * 2 + (1 - c)
            rows = pl.ds(pl.multiple_of(REACH * BLOCK + src_t * R, 64), R)
            rcopy(d.at[rows], d.at[rows], gs.at[it, 0], gr.at[it, src_t], partner()).wait_recv()

    def p_send(e):
        if e < 4:
            return rcopy(pts.at[e + 1, c], pbuf.at[e, c], pzs.at[e], pzr.at[e], {"rows": z + 1})
        return rcopy(pts.at[e - 9, c], pbuf.at[e, c], pzs.at[e], pzr.at[e], {"rows": z - 1})

    def can_send(e):
        if e < 4:
            return jnp.logical_and(has_next, e + 1 >= b0c + 1)
        return jnp.logical_and(has_prev, e - 9 <= b1c - 1)

    def p_fwd(e):
        return rcopy(pbuf.at[e, c], pbuf.at[e, c], pfs.at[e], pfr.at[e], partner())

    def d_unit(it, d, way, o, k, cc):
        g = 5 * (lax.rem(x + nx - o, nx) * 2 + cc) + k
        b = g // T
        needed = b >= b0c + 1 if way == 0 else b <= b1c - 1
        shift = -BLOCK if way == 0 else (REACH + 5) * BLOCK
        n = (way * nx + o) * 5 + k
        src = d.at[pl.ds(pl.multiple_of(g * U + REACH * BLOCK, 64), U)]
        dst = d.at[pl.ds(pl.multiple_of(jnp.where(needed, g * U + shift, 0), 64), U)]
        dev = {"rows": z + 1 if way == 0 else z - 1}
        can = jnp.logical_and(needed, has_next if way == 0 else has_prev)
        got = jnp.logical_and(needed, has_prev if way == 0 else has_next)
        return (can, got, lambda: rcopy(src, dst, dzs.at[it, n], dzr.at[it, n], dev),
                lambda: rcopy(dst, dst, dfs.at[it, n], dfr.at[it, n], partner()))

    def units(it, d, o, cc, which, fn):
        for k in range(5):
            for way in range(2):
                can, got, sent, passed = d_unit(it, d, way, o, k, cc)

                @pl.when(can if which == "can" else got)
                def _():
                    fn(sent, passed)

    def d_start(it, d, o):
        units(it, d, o, c, "can", lambda sent, passed: sent().start())

    def pfwd_in(e):
        v = pbuf.at[e, 1 - c]
        return rcopy(v, v, pfs.at[e], pfr.at[e], partner())

    def each(cond, fn):
        for e in EXT:
            @pl.when(cond(e))
            def _(e=e):
                fn(e)

    pc = [rcopy(pres.at[t], pres.at[t], prs.at[o], prr.at[t], dev) for o, _, dev in mates()]
    for cp in pc:
        cp.start()
    for cp in gather_copies(0, d0):
        cp.start()
    d_start(0, d0, 0)
    each(can_send, lambda e: p_send(e).start())
    lc.wait()

    for k in range(5):
        g = 5 * t + k
        hb = g // UPH
        off = pl.multiple_of(lax.rem(g, UPH) * U, U)
        rows = pbuf[4 + hb // 2, lax.rem(hb, 2), pl.ds(off, U), :].astype(f32)
        turned = pltpu.roll(rows, 64, 1)
        abuf[k * U:(k + 1) * U, 0:128] = (-2.0 * rows).astype(bf16)
        abuf[k * U:(k + 1) * U, 128:256] = (-2.0 * turned).astype(bf16)
        na[k * U:(k + 1) * U, :] = jnp.broadcast_to(
            jnp.sum(rows * (rows + turned), axis=1, keepdims=True), (U, 128))

    for o, ot, dev in mates():
        rcopy(pres.at[ot], pres.at[ot], prs.at[o], prr.at[ot], dev).wait_recv()
    own = pres[0]
    for i in range(1, T):
        own = own + pres[i]
    prevp[1] = jnp.where(lane >= 25, own, 0.0)
    prevp[2] = jnp.where(lane < 25, own, 0.0)

    def q_copy():
        return rcopy(prevp.at[2], prevp.at[0], qs, qr, {"rows": z + 1})

    @pl.when(has_next)
    def _():
        q_copy().start()

    @pl.when(jnp.logical_not(has_prev))
    def _():
        prevp[0] = jnp.zeros((8, 128), f32)

    def build(e, listed):
        for h in range(2):
            blk = pbuf[e, h]
            b = blk[:HALF]
            nr = blk[HALF:].astype(f32)
            nc = jnp.concatenate([nr[0:1] + nr[1:2] + nr[2:3], nr[3:4] + nr[4:5] + nr[5:6]], axis=1)
            gram = lax.dot_general(abuf[...], jnp.concatenate([b, b], axis=1),
                                   (((1,), (1,)), ((), ())), preferred_element_type=f32)
            for k in range(5):
                i = (5 * t + k) // T
                j = e - 4
                dist = jnp.abs(i - j)
                code = jnp.where(dist <= REACH, (jnp.minimum(i, j) + 5) * 5 + dist, 127)
                m = jnp.sum(jnp.where(lane == code, listed, 0.0), axis=1, keepdims=True)
                u = slice(k * U, (k + 1) * U)
                s = gram[u] + nc + na[u, 0:1]
                s = jnp.maximum(s, 1e-20)
                r = s * lax.rsqrt(s) * (1.0 / 12.0)
                base = jnp.maximum(m - r, 0.0)
                base2 = base * base
                kt = base2 * base2 * (4.0 * r + 1.0)
                kbuf[e - b0, u, h * HALF:(h + 1) * HALF] = kt.astype(bf16)

    def builds(lo, hi, listed):
        def body(e, carry):
            build(e, listed)
            return carry
        lax.fori_loop(lo, hi, body, 0)

    def mults(d, lo, hi):
        def body(e, carry):
            acc[...] += jnp.dot(kbuf[e - b0], d[pl.ds(pl.multiple_of(e * BLOCK, BLOCK), BLOCK), :],
                                preferred_element_type=f32)
            return carry
        lax.fori_loop(lo, hi, body, 0)

    prev_lo = jnp.where(has_prev, b0, 4)
    next_hi = jnp.where(has_next, b1 + 9, 9)

    own_list = jnp.minimum(prevp[1, 0:1], 1.0)
    acc[...] = jnp.zeros_like(acc)
    builds(4, 6, own_list)
    gather_forward(0, d0)
    builds(6, 7, own_list)
    gather_wait(0, d0)
    builds(7, 9, own_list)

    def p_take(e):
        p_send(e).wait_recv()
        p_fwd(e).start()

    each(have, p_take)
    mults(d0, 4, 9)

    @pl.when(has_prev)
    def _():
        q_copy().wait_recv()
    each(have, lambda e: pfwd_in(e).wait_recv())
    whole_list = jnp.minimum(prevp[1, 0:1] + prevp[0, 0:1], 1.0)
    builds(prev_lo, 4, whole_list)
    builds(9, next_hi, whole_list)

    def d_finish(it, d):
        def take(sent, passed):
            sent().wait_recv()
            passed().start()
        for o in range(nx):
            units(it, d, o, c, "got", take)
        for o in range(nx):
            units(it, d, o, 1 - c, "got", lambda sent, passed: passed().wait_recv())
        mults(d, prev_lo, 4)
        mults(d, 9, next_hi)

    d_finish(0, d0)

    def total(it, sums):
        rows = [*sums] + [jnp.zeros((8 - len(sums), 128), f32)]
        if flat:
            red1[it, me] = jnp.concatenate(rows, axis=0)
            v = red1.at[it, me]
            for o, m, dev in others():
                rcopy(v, v, r1s.at[it, o], r1r.at[it, me], dev).start()
            for o, m, dev in others():
                w = red1.at[it, m]
                rcopy(w, w, r1s.at[it, o], r1r.at[it, m], dev).wait_recv()
            a = red1[it, 0]
            for i in range(1, T * nz):
                a = a + red1[it, i]
            return a
        red1[it, t] = jnp.concatenate(rows, axis=0)
        v = red1.at[it, t]
        for o, ot, dev in mates():
            rcopy(v, v, r1s.at[it, o], r1r.at[it, t], dev).start()
        for o, ot, dev in mates():
            w = red1.at[it, ot]
            rcopy(w, w, r1s.at[it, o], r1r.at[it, ot], dev).wait_recv()
        a = red1[it, 0]
        for i in range(1, T):
            a = a + red1[it, i]
        red2[it, z] = a
        v = red2.at[it, z]
        for o, oz, dev in ranks():
            rcopy(v, v, r2s.at[it, o], r2r.at[it, z], dev).start()
        for o, oz, dev in ranks():
            w = red2.at[it, oz]
            rcopy(w, w, r2s.at[it, o], r2r.at[it, oz], dev).wait_recv()
        a = red2[it, 0]
        for i in range(1, nz):
            a = a + red2[it, i]
        return a

    def colsum(v):
        return jnp.sum(v, axis=0, keepdims=True)

    tv = tgt[...]
    q = 0.25 * tv + acc[...] * (1.0 / BLOCK)
    sums = total(0, (colsum(tv * tv), colsum(tv * q), colsum(q * q)))
    rr, tq, qq = sums[0:1], sums[1:2], sums[2:3]
    alpha = rr / tq
    beta = (alpha * alpha * qq - rr) / rr
    q = 0.25 * tgt[...] + acc[...] * (1.0 / BLOCK)
    first = tgt[...] - alpha * q
    r1[...] = first
    second = first + beta * tgt[...]
    dir2[...] = second
    d1[own_rows, :] = second.astype(bf16)
    for cp in gather_copies(1, d1):
        cp.start()
    d_start(1, d1, 0)
    acc[...] = jnp.zeros_like(acc)
    gather_forward(1, d1)
    gather_wait(1, d1)
    mults(d1, 4, 9)
    d_finish(1, d1)
    q = 0.25 * dir2[...] + acc[...] * (1.0 / BLOCK)
    sums = total(1, (colsum(r1[...] * r1[...]), colsum(dir2[...] * q)))
    alpha2 = sums[0:1] / sums[1:2]
    q = 0.25 * dir2[...] + acc[...] * (1.0 / BLOCK)
    sol[...] = alpha * tgt[...] + alpha2 * dir2[...]
    res[...] = r1[...] - alpha2 * q

    for cp in pc:
        cp.wait_send()

    @pl.when(has_next)
    def _():
        q_copy().wait_send()
    each(can_send, lambda e: p_send(e).wait_send())
    each(have, lambda e: p_fwd(e).wait_send())
    for it, d in enumerate((d0, d1)):
        for cp in gather_copies(it, d):
            cp.wait_send()
        for o in range(1, nx):
            gather_from(it, d, o)[1].wait_send()
        for o in range(nx):
            units(it, d, o, c, "can", lambda sent, passed: sent().wait_send())
            units(it, d, o, c, "got", lambda sent, passed: passed().wait_send())
        if flat:
            for o, m, dev in others():
                rcopy(red1.at[it, me], red1.at[it, me], r1s.at[it, o], r1r.at[it, me], dev).wait_send()
            continue
        for o, ot, dev in mates():
            rcopy(red1.at[it, t], red1.at[it, t], r1s.at[it, o], r1r.at[it, t], dev).wait_send()
        for o, oz, dev in ranks():
            rcopy(red2.at[it, z], red2.at[it, z], r2s.at[it, o], r2r.at[it, z], dev).wait_send()


def local(nz, nx, points, targets, pair_list):
    T = nx * 2
    n_red = T * nz if T * nz <= 16 else T
    R = targets.shape[0]
    pts = pack_points(points)
    dma = pltpu.SemaphoreType.DMA
    vmem = pl.BlockSpec(memory_space=pltpu.VMEM)
    shape = jax.ShapeDtypeStruct(targets.shape, f32)
    return pl.pallas_call(
        functools.partial(kernel, nz, nx, pair_list.shape[2]),
        out_shape=(shape, shape),
        in_specs=[vmem, pl.BlockSpec(memory_space=pl.ANY), pl.BlockSpec(memory_space=pltpu.SMEM)],
        out_specs=(vmem, vmem),
        scratch_shapes=[
            pltpu.VMEM((SLOTS, 2, HROWS, 128), bf16),
            pltpu.VMEM((SLOTS * BLOCK, 128), bf16),
            pltpu.VMEM((SLOTS * BLOCK, 128), bf16),
            pltpu.VMEM((10, R, BLOCK), bf16),
            pltpu.VMEM((R, 256), bf16),
            pltpu.VMEM((R, 128), f32),
            pltpu.VMEM((R, 128), f32),
            pltpu.VMEM((R, 128), f32),
            pltpu.VMEM((R, 128), f32),
            pltpu.VMEM((T, 8, 128), f32),
            pltpu.VMEM((3, 8, 128), f32),
            pltpu.VMEM((2, n_red, 8, 128), f32),
            pltpu.VMEM((2, nz, 8, 128), f32),
            dma,
            dma((2, nx)), dma((2, T)), dma((2, nx)),
            dma((SLOTS,)), dma((SLOTS,)), dma((SLOTS,)), dma((SLOTS,)),
            dma((2, 10 * nx)), dma((2, 10 * nx)), dma((2, 10 * nx)), dma((2, 10 * nx)),
            dma((T,)), dma((T,)), dma, dma,
            dma((2, n_red)), dma((2, n_red)), dma((2, nz)), dma((2, nz)),
        ],
        compiler_params=pltpu.CompilerParams(
            collective_id=0, has_side_effects=True, vmem_limit_bytes=48 * 1024 * 1024),
        cost_estimate=pl.CostEstimate(flops=5 * 10**9, bytes_accessed=2 * 10**6, transcendentals=3 * 10**6),
    )(targets, pts, pair_list)


def solution(mesh):
    nz, nx = mesh.shape["rows"], mesh.shape["tiles"]
    in_specs = (
        P(("groups", "rows"), None),
        P(("groups", "rows", "tiles", "sub"), None),
        P(("groups", "rows", "tiles", "sub"), None, None),
    )
    out_specs = (
        P(("groups", "rows", "tiles", "sub"), None),
        P(("groups", "rows", "tiles", "sub"), None),
    )
    return jax.shard_map(functools.partial(local, nz, nx), mesh=mesh, in_specs=in_specs,
                         out_specs=out_specs, check_vma=False)
```

```python
import functools

import jax
import jax.numpy as jnp
from jax import lax
from jax.experimental import pallas as pl
from jax.experimental.pallas import tpu as pltpu
from jax.sharding import PartitionSpec as P

BLOCK = 512
HALF = 256
HROWS = 272
REACH = 4
SLOTS = 13
f32 = jnp.float32
bf16 = jnp.bfloat16


def split(v):
    hi = lax.reduce_precision(v, 8, 7)
    return hi, v - hi


def pack_points(points):
    hi, rest = split(points)
    lo = lax.reduce_precision(rest, 8, 7)
    both = hi + lo
    sq = jnp.sum(both * both, axis=1)
    n1, rest = split(sq)
    n2, n3 = split(rest)
    blocks = points.shape[0] // BLOCK
    feats = jnp.concatenate([hi, lo], axis=1).astype(bf16).reshape(blocks, 2, HALF, 128)
    pieces = jnp.stack([n1, n2, n3], axis=0).reshape(3, blocks, 2, 2, 128)
    pieces = pieces.transpose(1, 2, 3, 0, 4).reshape(blocks, 2, 6, 128)
    pieces = jnp.pad(pieces, ((0, 0), (0, 0), (0, 10), (0, 0))).astype(bf16)
    return jnp.concatenate([feats, pieces], axis=2)


def kernel(nz, nx, cap, tgt, pts, pairs, sol, res, pbuf, d0, d1, kbuf, abuf, na, acc, r1, dir2,
           pres, prevp, red1, red2, loc, gs, gr, gf, pzs, pzr, pfs, pfr, dzs, dzr, dfs, dfr,
           prs, prr, qs, qr, r1s, r1r, r2s, r2r):
    T = nx * 2
    R = tgt.shape[0]
    U = BLOCK // T
    UPH = T // 2
    x = lax.axis_index("tiles")
    c = lax.axis_index("sub")
    z = lax.axis_index("rows")
    t = x * 2 + c
    b0 = (5 * t) // T
    b1 = (5 * t + 4) // T
    b0c = (10 * x) // T
    b1c = (10 * x + 9) // T
    has_prev = z > 0
    has_next = z < nz - 1

    def partner():
        return {"sub": 1 - c}

    def have(e):
        if e < 4:
            return jnp.logical_and(has_prev, e + 1 >= b0c + 1)
        return jnp.logical_and(has_next, e - 9 <= b1c - 1)

    def rcopy(src, dst, s, r, dev):
        return pltpu.make_async_remote_copy(
            src_ref=src, dst_ref=dst, send_sem=s, recv_sem=r, device_id=dev,
            device_id_type=pl.DeviceIdType.MESH)

    EXT = (3, 9, 2, 10, 1, 11, 0, 12)

    bar = pltpu.get_barrier_semaphore()

    def mates():
        for o in range(1, T):
            ot = lax.rem(t + o, T)
            yield o, ot, {"tiles": ot // 2, "sub": lax.rem(ot, 2)}

    def ranks():
        for o in range(1, nz):
            oz = lax.rem(z + o, nz)
            yield o, oz, {"rows": oz}

    flat = T * nz <= 16
    me = z * T + t

    def others():
        for o in range(1, T * nz):
            m = lax.rem(me + o, T * nz)
            yield o, m, {"rows": m // T, "tiles": lax.rem(m, T) // 2, "sub": lax.rem(m, 2)}

    greeted = list(others()) if flat else [*mates(), *ranks()]
    for _, _, dev in greeted:
        pl.semaphore_signal(bar, inc=1, device_id=dev, device_id_type=pl.DeviceIdType.MESH)

    own_rows = pl.ds(pl.multiple_of(REACH * BLOCK + t * R, 64), R)
    lc = pltpu.make_async_copy(pts, pbuf.at[pl.ds(4, 5)], loc)
    lc.start()
    d0[own_rows, :] = tgt[...].astype(bf16)
    lane = lax.broadcasted_iota(jnp.int32, (1, 128), 1)
    mine = jnp.zeros((1, 128), f32)
    for k in range(cap):
        left = pairs[0, 0, k]
        right = pairs[0, 1, k]
        code = jnp.where(left >= 0, (left - z * 5) * 5 + right - left, -100)
        hit = jnp.logical_or(lane == code, lane == code + 25)
        mine = jnp.where(hit, 1.0, mine)
    pres[t] = jnp.broadcast_to(mine, (8, 128))

    pl.semaphore_wait(bar, len(greeted))

    def gather_copies(it, d):
        view = d.at[own_rows]
        out = [rcopy(view, view, gs.at[it, 0], gr.at[it, t], partner())]
        for o in range(1, nx):
            out.append(rcopy(view, view, gs.at[it, o], gr.at[it, t], {"tiles": lax.rem(x + o, nx)}))
        return out

    def gather_from(it, d, o):
        src_t = lax.rem(x + nx - o, nx) * 2 + c
        rows = pl.ds(pl.multiple_of(REACH * BLOCK + src_t * R, 64), R)
        return (rcopy(d.at[rows], d.at[rows], gs.at[it, o], gr.at[it, src_t], partner()),
                rcopy(d.at[rows], d.at[rows], gf.at[it, o], gr.at[it, src_t], partner()))

    def gather_forward(it, d):
        for o in range(1, nx):
            inn, fwd = gather_from(it, d, o)
            inn.wait_recv()
            fwd.start()
            d_start(it, d, o)

    def gather_wait(it, d):
        for xx in range(nx):
            src_t = xx * 2 + (1 - c)
            rows = pl.ds(pl.multiple_of(REACH * BLOCK + src_t * R, 64), R)
            rcopy(d.at[rows], d.at[rows], gs.at[it, 0], gr.at[it, src_t], partner()).wait_recv()

    def p_send(e):
        if e < 4:
            return rcopy(pts.at[e + 1, c], pbuf.at[e, c], pzs.at[e], pzr.at[e], {"rows": z + 1})
        return rcopy(pts.at[e - 9, c], pbuf.at[e, c], pzs.at[e], pzr.at[e], {"rows": z - 1})

    def can_send(e):
        if e < 4:
            return jnp.logical_and(has_next, e + 1 >= b0c + 1)
        return jnp.logical_and(has_prev, e - 9 <= b1c - 1)

    def p_fwd(e):
        return rcopy(pbuf.at[e, c], pbuf.at[e, c], pfs.at[e], pfr.at[e], partner())

    def d_unit(it, d, way, o, k, cc):
        g = 5 * (lax.rem(x + nx - o, nx) * 2 + cc) + k
        b = g // T
        needed = b >= b0c + 1 if way == 0 else b <= b1c - 1
        shift = -BLOCK if way == 0 else (REACH + 5) * BLOCK
        n = (way * nx + o) * 5 + k
        src = d.at[pl.ds(pl.multiple_of(g * U + REACH * BLOCK, 64), U)]
        dst = d.at[pl.ds(pl.multiple_of(jnp.where(needed, g * U + shift, 0), 64), U)]
        dev = {"rows": z + 1 if way == 0 else z - 1}
        can = jnp.logical_and(needed, has_next if way == 0 else has_prev)
        got = jnp.logical_and(needed, has_prev if way == 0 else has_next)
        return (can, got, lambda: rcopy(src, dst, dzs.at[it, n], dzr.at[it, n], dev),
                lambda: rcopy(dst, dst, dfs.at[it, n], dfr.at[it, n], partner()))

    def units(it, d, o, cc, which, fn):
        for k in range(5):
            for way in range(2):
                can, got, sent, passed = d_unit(it, d, way, o, k, cc)

                @pl.when(can if which == "can" else got)
                def _():
                    fn(sent, passed)

    def d_start(it, d, o):
        units(it, d, o, c, "can", lambda sent, passed: sent().start())

    def pfwd_in(e):
        v = pbuf.at[e, 1 - c]
        return rcopy(v, v, pfs.at[e], pfr.at[e], partner())

    def each(cond, fn):
        for e in EXT:
            @pl.when(cond(e))
            def _(e=e):
                fn(e)

    pc = [rcopy(pres.at[t], pres.at[t], prs.at[o], prr.at[t], dev) for o, _, dev in mates()]
    for cp in pc:
        cp.start()
    for cp in gather_copies(0, d0):
        cp.start()
    d_start(0, d0, 0)
    each(can_send, lambda e: p_send(e).start())
    lc.wait()

    for k in range(5):
        g = 5 * t + k
        hb = g // UPH
        off = pl.multiple_of(lax.rem(g, UPH) * U, U)
        rows = pbuf[4 + hb // 2, lax.rem(hb, 2), pl.ds(off, U), :].astype(f32)
        turned = pltpu.roll(rows, 64, 1)
        abuf[k * U:(k + 1) * U, 0:128] = (-2.0 * rows).astype(bf16)
        abuf[k * U:(k + 1) * U, 128:256] = (-2.0 * turned).astype(bf16)
        na[k * U:(k + 1) * U, :] = jnp.broadcast_to(
            jnp.sum(rows * (rows + turned), axis=1, keepdims=True), (U, 128))

    for o, ot, dev in mates():
        rcopy(pres.at[ot], pres.at[ot], prs.at[o], prr.at[ot], dev).wait_recv()
    own = pres[0]
    for i in range(1, T):
        own = own + pres[i]
    prevp[1] = jnp.where(lane >= 25, own, 0.0)
    prevp[2] = jnp.where(lane < 25, own, 0.0)

    def q_copy():
        return rcopy(prevp.at[2], prevp.at[0], qs, qr, {"rows": z + 1})

    @pl.when(has_next)
    def _():
        q_copy().start()

    @pl.when(jnp.logical_not(has_prev))
    def _():
        prevp[0] = jnp.zeros((8, 128), f32)

    def build(e, listed):
        for h in range(2):
            blk = pbuf[e, h]
            b = blk[:HALF]
            nr = blk[HALF:].astype(f32)
            nc = jnp.concatenate([nr[0:1] + nr[1:2] + nr[2:3], nr[3:4] + nr[4:5] + nr[5:6]], axis=1)
            gram = lax.dot_general(abuf[...], jnp.concatenate([b, b], axis=1),
                                   (((1,), (1,)), ((), ())), preferred_element_type=f32)
            for k in range(5):
                i = (5 * t + k) // T
                j = e - 4
                dist = jnp.abs(i - j)
                code = jnp.where(dist <= REACH, (jnp.minimum(i, j) + 5) * 5 + dist, 127)
                m = jnp.sum(jnp.where(lane == code, listed, 0.0), axis=1, keepdims=True)
                u = slice(k * U, (k + 1) * U)
                s = gram[u] + nc + na[u, 0:1]
                s = jnp.maximum(s, 1e-20)
                r = s * lax.rsqrt(s) * (1.0 / 12.0)
                base = jnp.maximum(m - r, 0.0)
                base2 = base * base
                kt = base2 * base2 * (4.0 * r + 1.0)
                kbuf[e - b0, u, h * HALF:(h + 1) * HALF] = kt.astype(bf16)

    def builds(lo, hi, listed):
        def body(e, carry):
            build(e, listed)
            return carry
        lax.fori_loop(lo, hi, body, 0)

    def mults(d, lo, hi):
        def body(e, carry):
            acc[...] += jnp.dot(kbuf[e - b0], d[pl.ds(pl.multiple_of(e * BLOCK, BLOCK), BLOCK), :],
                                preferred_element_type=f32)
            return carry
        lax.fori_loop(lo, hi, body, 0)

    prev_lo = jnp.where(has_prev, b0, 4)
    next_hi = jnp.where(has_next, b1 + 9, 9)

    own_list = jnp.minimum(prevp[1, 0:1], 1.0)
    acc[...] = jnp.zeros_like(acc)
    builds(4, 6, own_list)
    gather_forward(0, d0)
    builds(6, 7, own_list)
    gather_wait(0, d0)
    builds(7, 9, own_list)

    def p_take(e):
        p_send(e).wait_recv()
        p_fwd(e).start()

    each(have, p_take)
    mults(d0, 4, 9)

    @pl.when(has_prev)
    def _():
        q_copy().wait_recv()
    each(have, lambda e: pfwd_in(e).wait_recv())
    whole_list = jnp.minimum(prevp[1, 0:1] + prevp[0, 0:1], 1.0)
    builds(prev_lo, 4, whole_list)
    builds(9, next_hi, whole_list)

    def d_finish(it, d):
        def take(sent, passed):
            sent().wait_recv()
            passed().start()
        for o in range(nx):
            units(it, d, o, c, "got", take)
        for o in range(nx):
            units(it, d, o, 1 - c, "got", lambda sent, passed: passed().wait_recv())
        mults(d, prev_lo, 4)
        mults(d, 9, next_hi)

    d_finish(0, d0)

    def total(it, sums):
        rows = [*sums] + [jnp.zeros((8 - len(sums), 128), f32)]
        if flat:
            red1[it, me] = jnp.concatenate(rows, axis=0)
            v = red1.at[it, me]
            for o, m, dev in others():
                rcopy(v, v, r1s.at[it, o], r1r.at[it, me], dev).start()
            for o, m, dev in others():
                w = red1.at[it, m]
                rcopy(w, w, r1s.at[it, o], r1r.at[it, m], dev).wait_recv()
            a = red1[it, 0]
            for i in range(1, T * nz):
                a = a + red1[it, i]
            return a
        red1[it, t] = jnp.concatenate(rows, axis=0)
        v = red1.at[it, t]
        for o, ot, dev in mates():
            rcopy(v, v, r1s.at[it, o], r1r.at[it, t], dev).start()
        for o, ot, dev in mates():
            w = red1.at[it, ot]
            rcopy(w, w, r1s.at[it, o], r1r.at[it, ot], dev).wait_recv()
        a = red1[it, 0]
        for i in range(1, T):
            a = a + red1[it, i]
        red2[it, z] = a
        v = red2.at[it, z]
        for o, oz, dev in ranks():
            rcopy(v, v, r2s.at[it, o], r2r.at[it, z], dev).start()
        for o, oz, dev in ranks():
            w = red2.at[it, oz]
            rcopy(w, w, r2s.at[it, o], r2r.at[it, oz], dev).wait_recv()
        a = red2[it, 0]
        for i in range(1, nz):
            a = a + red2[it, i]
        return a

    def colsum(v):
        return jnp.sum(v, axis=0, keepdims=True)

    tv = tgt[...]
    q = 0.25 * tv + acc[...] * (1.0 / BLOCK)
    sums = total(0, (colsum(tv * tv), colsum(tv * q), colsum(q * q)))
    rr, tq, qq = sums[0:1], sums[1:2], sums[2:3]
    alpha = rr / tq
    beta = (alpha * alpha * qq - rr) / rr
    q = 0.25 * tgt[...] + acc[...] * (1.0 / BLOCK)
    first = tgt[...] - alpha * q
    r1[...] = first
    second = first + beta * tgt[...]
    dir2[...] = second
    d1[own_rows, :] = second.astype(bf16)
    for cp in gather_copies(1, d1):
        cp.start()
    d_start(1, d1, 0)
    acc[...] = jnp.zeros_like(acc)
    gather_forward(1, d1)
    gather_wait(1, d1)
    mults(d1, 4, 9)
    d_finish(1, d1)
    q = 0.25 * dir2[...] + acc[...] * (1.0 / BLOCK)
    sums = total(1, (colsum(r1[...] * r1[...]), colsum(dir2[...] * q)))
    alpha2 = sums[0:1] / sums[1:2]
    q = 0.25 * dir2[...] + acc[...] * (1.0 / BLOCK)
    sol[...] = alpha * tgt[...] + alpha2 * dir2[...]
    res[...] = r1[...] - alpha2 * q

    for cp in pc:
        cp.wait_send()

    @pl.when(has_next)
    def _():
        q_copy().wait_send()
    each(can_send, lambda e: p_send(e).wait_send())
    each(have, lambda e: p_fwd(e).wait_send())
    for it, d in enumerate((d0, d1)):
        for cp in gather_copies(it, d):
            cp.wait_send()
        for o in range(1, nx):
            gather_from(it, d, o)[1].wait_send()
        for o in range(nx):
            units(it, d, o, c, "can", lambda sent, passed: sent().wait_send())
            units(it, d, o, c, "got", lambda sent, passed: passed().wait_send())
        if flat:
            for o, m, dev in others():
                rcopy(red1.at[it, me], red1.at[it, me], r1s.at[it, o], r1r.at[it, me], dev).wait_send()
            continue
        for o, ot, dev in mates():
            rcopy(red1.at[it, t], red1.at[it, t], r1s.at[it, o], r1r.at[it, t], dev).wait_send()
        for o, oz, dev in ranks():
            rcopy(red2.at[it, z], red2.at[it, z], r2s.at[it, o], r2r.at[it, z], dev).wait_send()


def local(nz, nx, points, targets, pair_list):
    T = nx * 2
    n_red = T * nz if T * nz <= 16 else T
    R = targets.shape[0]
    pts = pack_points(points)
    dma = pltpu.SemaphoreType.DMA
    vmem = pl.BlockSpec(memory_space=pltpu.VMEM)
    shape = jax.ShapeDtypeStruct(targets.shape, f32)
    return pl.pallas_call(
        functools.partial(kernel, nz, nx, pair_list.shape[2]),
        out_shape=(shape, shape),
        in_specs=[vmem, pl.BlockSpec(memory_space=pl.ANY), pl.BlockSpec(memory_space=pltpu.SMEM)],
        out_specs=(vmem, vmem),
        scratch_shapes=[
            pltpu.VMEM((SLOTS, 2, HROWS, 128), bf16),
            pltpu.VMEM((SLOTS * BLOCK, 128), bf16),
            pltpu.VMEM((SLOTS * BLOCK, 128), bf16),
            pltpu.VMEM((10, R, BLOCK), bf16),
            pltpu.VMEM((R, 256), bf16),
            pltpu.VMEM((R, 128), f32),
            pltpu.VMEM((R, 128), f32),
            pltpu.VMEM((R, 128), f32),
            pltpu.VMEM((R, 128), f32),
            pltpu.VMEM((T, 8, 128), f32),
            pltpu.VMEM((3, 8, 128), f32),
            pltpu.VMEM((2, n_red, 8, 128), f32),
            pltpu.VMEM((2, nz, 8, 128), f32),
            dma,
            dma((2, nx)), dma((2, T)), dma((2, nx)),
            dma((SLOTS,)), dma((SLOTS,)), dma((SLOTS,)), dma((SLOTS,)),
            dma((2, 10 * nx)), dma((2, 10 * nx)), dma((2, 10 * nx)), dma((2, 10 * nx)),
            dma((T,)), dma((T,)), dma, dma,
            dma((2, n_red)), dma((2, n_red)), dma((2, nz)), dma((2, nz)),
        ],
        compiler_params=pltpu.CompilerParams(
            collective_id=0, has_side_effects=True, vmem_limit_bytes=48 * 1024 * 1024),
        cost_estimate=pl.CostEstimate(flops=5 * 10**9, bytes_accessed=2 * 10**6, transcendentals=3 * 10**6),
    )(targets, pts, pair_list)


def solution(mesh):
    nz, nx = mesh.shape["rows"], mesh.shape["tiles"]
    in_specs = (
        P(("groups", "rows"), None),
        P(("groups", "rows", "tiles", "sub"), None),
        P(("groups", "rows", "tiles", "sub"), None, None),
    )
    out_specs = (
        P(("groups", "rows", "tiles", "sub"), None),
        P(("groups", "rows", "tiles", "sub"), None),
    )
    return jax.shard_map(functools.partial(local, nz, nx), mesh=mesh, in_specs=in_specs,
                         out_specs=out_specs, check_vma=False)
```
